32 devices in a mesh: ctx: 8 (over z, core), tp: 4 (over y, x).
Axes of the slice: x: 2, y: 2, z: 4, core: 2. Of those that a mesh axis runs over, the one named last changes fastest.
Arguments:
- queries: bfloat16 [512, 4096], P('ctx', 'tp'), may hold values from -6 to 6
- keys: bfloat16 [512, 256], P('ctx'), may hold values from -6 to 6
- values: bfloat16 [512, 256], P('ctx'), may hold values from -6 to 6
- resid: bfloat16 [512, 4096], P(('ctx', 'tp')), may hold values from -4 to 4
- out_proj: bfloat16 [4096, 4096], P('tp'), may hold values from -0.375 to 0.375
- norm_gain: float32 [4096], replicated, may hold values from 0.1 to 1.9
- expert_ids: int32 [512, 8], P(('ctx', 'tp')), may hold values from 0 to 15, all different within a row; in each aligned block of 16 rows (0 to 15, 16 to 31, ...) at most 10 rows name the same one
- gates: float32 [512, 8], P(('ctx', 'tp')), may hold values from 0.1 to 0.5
- w_gate: bfloat16 [16, 1536, 4096], P('ctx', 'tp'), may hold values from -0.09375 to 0.09375
- w_up: bfloat16 [16, 1536, 4096], P('ctx', 'tp'), may hold values from -0.09375 to 0.09375
- w_down: bfloat16 [16, 1536, 4096], P('ctx', 'tp'), may hold values from -0.15625 to 0.15625
- cotangent: bfloat16 [512, 4096], P(('ctx', 'tp')), may hold values from -2 to 2
Outputs:
- layer_out: bfloat16 [512, 4096], P(('ctx', 'tp'))
- grad_gate: bfloat16 [16, 1536, 4096], P('ctx', 'tp')
- grad_up: bfloat16 [16, 1536, 4096], P('ctx', 'tp')
- grad_down: bfloat16 [16, 1536, 4096], P('ctx', 'tp')
The draws below stay inside these ranges and needn't reach their ends.
Inputs may be any that keep to these rules, and one draw needn't show every extreme that they name: `expert_ids`: in the 16 rows of one device (aligned blocks of rows) no expert is named more than 10 times, a bound that some block reaches; each row names 8 different experts.
All inputs are finite; a program needn't handle non-finite values.
Results may differ from the reference program's by a relative error of at most 0.025.
Values may be sent and summed in bfloat16 or wider, within the bound.
A program may use at most 192 MiB of HBM per device.

```python
import math
import jax
import jax.numpy as jnp
import numpy as np
from jax import lax

D = 4096
FF = 1536
QHEADS = 32
KVHEADS = 2
HEAD = 128
TOPK = 8
ROWS = 16
TOKENS = 512
EXPERTS = 16
CAP = 10
N_CTX = 8
N_TP = 4


def draw_queries(key, part):
    key = jax.random.fold_in(key, 11)
    drawn = jnp.clip(jax.random.normal(key, (TOKENS, QHEADS, HEAD), jnp.float32), -5.0, 5.0)
    return drawn.reshape(TOKENS, QHEADS * HEAD).astype(jnp.bfloat16)


def draw_keys(key, part):
    key = jax.random.fold_in(key, 12)
    drawn = jnp.clip(jax.random.normal(key, (TOKENS, KVHEADS, HEAD), jnp.float32), -5.0, 5.0)
    return drawn.reshape(TOKENS, KVHEADS * HEAD).astype(jnp.bfloat16)


def steps_of(stream_key, shape, cuts, low, high):
    level, own = 1.0, jax.random.fold_in(stream_key, 6)
    for axis_at, blocks in cuts:
        steps = jnp.exp(jax.random.uniform(jax.random.fold_in(own, axis_at), (blocks,), jnp.float32, low / len(cuts), high / len(cuts)))
        level = level * jnp.repeat(steps, shape[axis_at] // blocks).reshape([-1 if axis == axis_at else 1 for axis in range(len(shape))])
    return level


def assign_block(stream_key, own, number, rows, amount, top, bound, skew):
    ranking = jax.random.permutation(stream_key, amount)
    packed, ordinary = shares(amount, rows * top, bound, skew, True), shares(amount, rows * top, bound, skew, False)
    places = jnp.arange(amount)

    def named(sizes, rotation):
        used = int((sizes > 0).sum())
        fixed = max(1, used // 4)
        passed = fixed + (places - fixed + rotation * (used - fixed)) % max(1, amount - fixed)
        return jnp.zeros((amount,), jnp.int32).at[ranking[jnp.where(places < fixed, places, passed)]].set(jnp.asarray(sizes, jnp.int32))

    sizes = jnp.where(number % 4 == 0, named(packed, number // 4), named(ordinary, number - number // 4 - 1))
    mixed = jax.random.permutation(jax.random.fold_in(own, 3), amount)
    source_of, receiver = mixed[0:amount // 2 * 2:2], mixed[1:amount // 2 * 2:2]
    slack = jnp.minimum(sizes[source_of] - 1, bound - sizes[receiver]) // 2
    slack = jnp.where((source_of == ranking[0]) | (receiver == ranking[0]) | (sizes[receiver] == 0), 0, jnp.maximum(slack, 0))
    passed = jax.random.randint(jax.random.fold_in(own, 4), (amount // 2,), 0, 1 << 20) % (slack + 1)
    sizes = sizes.at[source_of].add(-passed).at[receiver].add(passed)
    items = jnp.searchsorted(jnp.cumsum(sizes), jnp.arange(rows * top), side="right").astype(jnp.int32)
    grid = items.reshape(top, rows).T
    grid = grid[jax.random.permutation(jax.random.fold_in(own, 1), rows)]
    rotation = jax.random.randint(jax.random.fold_in(own, 2), (rows, 1), 0, top)
    return jnp.take_along_axis(grid, (jnp.arange(top)[None, :] + rotation) % top, axis=1)


def shares(count, total, limit, skew, full):
    weights = [(1 << 20) // math.isqrt(grade ** skew) + 1 for grade in range(1, count + 1)]
    largest = limit if full else min(limit, max(-(-total // count), total * weights[0] // sum(weights)))
    least = 1 if total - largest >= count - 1 else 0
    given, rest = [largest] + [least] * (count - 1), total - largest - least * (count - 1)
    while rest > 0:
        free = [i for i in range(1, count) if given[i] < largest] or [i for i in range(1, count) if given[i] < limit]
        pool, remaining = sum([weights[i] for i in free]), rest
        for i in free:
            more = min(limit - given[i], max(1, remaining * weights[i] // pool), rest)
            given[i] = given[i] + more
            rest = rest - more
    return np.array(given)


def gaussian(rng, extent, scale, limit, shards=(), held_as=jnp.bfloat16):
    level = steps_of(rng, extent, shards, -0.22, 0.18) if shards else 1.0
    values = jax.random.normal(rng, extent, jnp.float32) * scale * level
    return jnp.minimum(jnp.maximum(values, -limit), limit).astype(held_as)


def setup_inputs(seed: int = 0) -> dict:
    key_list = jax.random.split(jax.random.key(seed), 13)
    queries = draw_queries(jax.random.fold_in(key_list[12], 71), 0)
    keys = draw_keys(jax.random.fold_in(key_list[12], 71), 0)
    values = gaussian(key_list[2], (TOKENS, KVHEADS * HEAD), 1.0, 6.0, ((0, 8),))
    resid = gaussian(key_list[3], (TOKENS, D), 0.5, 4.0, ((0, 32),))
    out_proj = gaussian(key_list[4], (QHEADS * HEAD, D), (QHEADS * HEAD // 16) ** -0.5, 0.375, ((0, 4),))
    norm_gain = jnp.clip(1.0 + 0.18 * jax.random.normal(key_list[5], (D,), jnp.float32), 0.1, 1.9)
    expert_ids_keys = jax.random.split(jax.random.fold_in(key_list[6], 1), TOKENS // ROWS)
    expert_ids_turns = jax.random.permutation(jax.random.fold_in(key_list[6], 3), TOKENS // ROWS)
    expert_ids = jax.vmap(lambda own, number: assign_block(jax.random.fold_in(key_list[6], 2), own, number, ROWS, EXPERTS, TOPK, CAP, 0))(expert_ids_keys, expert_ids_turns).reshape((TOKENS, TOPK))
    gates = jnp.clip(0.1 + 0.4 * jax.random.uniform(key_list[7], (TOKENS, TOPK), jnp.float32) ** steps_of(key_list[7], (TOKENS, TOPK), ((0, 32),), -0.2, 0.2), 0.1, 0.5)
    w_gate = gaussian(key_list[8], (EXPERTS, FF, D), D ** -0.5, 0.09375, ((0, 8), (1, 4)))
    w_up = gaussian(key_list[9], (EXPERTS, FF, D), D ** -0.5, 0.09375, ((0, 8), (1, 4)))
    w_down = gaussian(key_list[10], (EXPERTS, FF, D), FF ** -0.5, 0.15625, ((0, 8), (1, 4)))
    cotangent = gaussian(key_list[11], (TOKENS, D), 0.3, 2.0, ((0, 32),))
    return {"queries": queries, "keys": keys, "values": values, "resid": resid, "out_proj": out_proj, "norm_gain": norm_gain, "expert_ids": expert_ids, "gates": gates, "w_gate": w_gate, "w_up": w_up, "w_down": w_down, "cotangent": cotangent}


def reference(queries, keys, values, resid, out_proj, norm_gain, expert_ids, gates, w_gate, w_up, w_down, cotangent):
    tokens = queries.shape[0]
    group_size = QHEADS // KVHEADS
    score_scale = 1.0 / math.sqrt(HEAD)
    positions = jnp.arange(tokens, dtype=jnp.int32)
    visible = positions[None, :] <= positions[:, None]

    def one_head(head_index):
        query_head = lax.dynamic_slice_in_dim(queries, head_index * HEAD, HEAD, 1)
        kv_index = head_index // group_size
        key_head = lax.dynamic_slice_in_dim(keys, kv_index * HEAD, HEAD, 1)
        value_head = lax.dynamic_slice_in_dim(values, kv_index * HEAD, HEAD, 1)
        scores = jnp.dot(query_head, key_head.T, preferred_element_type=jnp.float32) * score_scale
        row_max = lax.optimization_barrier(jnp.max(jnp.where(visible, scores, -1e+30), axis=1, keepdims=True))
        probs = jnp.where(visible, jnp.exp(scores - row_max), 0.0)
        output = jnp.dot(probs.astype(jnp.bfloat16), value_head, preferred_element_type=jnp.float32)
        return (output / lax.optimization_barrier(jnp.sum(probs, axis=1, keepdims=True))).astype(jnp.bfloat16)
    heads_out = lax.map(one_head, jnp.arange(QHEADS, dtype=jnp.int32))
    attn = jnp.transpose(heads_out, (1, 0, 2)).reshape(tokens, QHEADS * HEAD)
    stream = resid.astype(jnp.float32) + jnp.dot(attn, out_proj, preferred_element_type=jnp.float32)
    normed = (stream * lax.rsqrt(lax.optimization_barrier(jnp.mean(stream * stream, axis=1, keepdims=True)) + 1e-06) * norm_gain).astype(jnp.bfloat16)
    pad_rows = jnp.concatenate([normed, jnp.zeros((1, D), jnp.bfloat16)], axis=0)
    pad_grads = jnp.concatenate([cotangent.astype(jnp.float32), jnp.zeros((1, D), jnp.float32)], axis=0)
    row_limit = N_CTX * N_TP * CAP
    ff_block = FF // N_TP

    def per_expert(accumulator, expert_index):
        hit_mask = expert_ids == expert_index
        route_weight = lax.optimization_barrier(jnp.sum(jnp.where(hit_mask, gates, 0.0), axis=1))
        chosen = jnp.any(hit_mask, axis=1)
        picked = jnp.nonzero(chosen, size=row_limit, fill_value=tokens)[0].astype(jnp.int32)
        expert_rows = pad_rows[picked]
        row_weight = jnp.concatenate([route_weight, jnp.zeros((1,), jnp.float32)])[picked]
        gate_matrix = lax.dynamic_index_in_dim(w_gate, expert_index, 0, keepdims=False)
        up_matrix = lax.dynamic_index_in_dim(w_up, expert_index, 0, keepdims=False)
        down_matrix = lax.dynamic_index_in_dim(w_down, expert_index, 0, keepdims=False)
        gate_val = jnp.dot(expert_rows, gate_matrix.T, preferred_element_type=jnp.float32)
        up_val = jnp.dot(expert_rows, up_matrix.T, preferred_element_type=jnp.float32)
        sigmoid_val = jax.nn.sigmoid(gate_val)
        silu_val = gate_val * sigmoid_val
        activated = (silu_val * up_val).astype(jnp.bfloat16)
        act_blocks = activated.astype(jnp.float32).reshape(row_limit, N_TP, ff_block)
        down_blocks = down_matrix.astype(jnp.float32).reshape(N_TP, ff_block, D)
        block_out = jnp.einsum('nbf,bfd->nbd', act_blocks, down_blocks, precision=lax.Precision.HIGHEST).astype(jnp.bfloat16)
        block_out = lax.optimization_barrier(block_out)
        expert_out = lax.optimization_barrier(jnp.sum(block_out.astype(jnp.float32), axis=1)).astype(jnp.bfloat16)
        accumulator = accumulator.at[picked].add(row_weight[:, None] * expert_out.astype(jnp.float32))
        grad_rows = (row_weight[:, None] * pad_grads[picked]).astype(jnp.bfloat16)
        back_act = jnp.dot(grad_rows, down_matrix.T, preferred_element_type=jnp.float32)
        d_gate = (back_act * up_val * sigmoid_val * (1.0 + gate_val * (1.0 - sigmoid_val))).astype(jnp.bfloat16)
        d_up = (back_act * silu_val).astype(jnp.bfloat16)
        grad_down = jnp.dot(activated.T, grad_rows, preferred_element_type=jnp.float32).astype(jnp.bfloat16)
        grad_gate = jnp.dot(d_gate.T, expert_rows, preferred_element_type=jnp.float32).astype(jnp.bfloat16)
        grad_up = jnp.dot(d_up.T, expert_rows, preferred_element_type=jnp.float32).astype(jnp.bfloat16)
        return (accumulator, (grad_gate, grad_up, grad_down))
    moe_sum, gradients = lax.scan(per_expert, jnp.zeros((tokens + 1, D), jnp.float32), jnp.arange(EXPERTS, dtype=jnp.int32))
    layer_out = (stream + moe_sum[:tokens]).astype(jnp.bfloat16)
    return (layer_out, gradients[0], gradients[1], gradients[2])
```

```python
import math

import jax
import jax.numpy as jnp
from jax import lax
from jax.sharding import PartitionSpec as P

D = 4096
QHEADS = 32
KVHEADS = 2
HEAD = 128
TOPK = 8


def shards(
    queries,
    keys,
    values,
    resid,
    out_proj,
    norm_gain,
    expert_ids,
    gates,
    w_gate,
    w_up,
    w_down,
    cotangent,
):
    groups = lax.axis_size("ctx")
    tensor = lax.axis_size("tp")
    tok_ctx = queries.shape[0]
    heads_dev = queries.shape[1] // HEAD
    group_size = QHEADS // KVHEADS
    kv_head = lax.axis_index("tp") * heads_dev // group_size
    key_mine = lax.dynamic_slice_in_dim(keys, kv_head * HEAD, HEAD, 1)
    value_mine = lax.dynamic_slice_in_dim(values, kv_head * HEAD, HEAD, 1)
    query_pos = lax.axis_index("ctx") * tok_ctx + jnp.arange(tok_ctx, dtype=jnp.int32)
    query_heads = queries.reshape(tok_ctx, heads_dev, HEAD)
    score_scale = 1.0 / math.sqrt(HEAD)
    running = jnp.full((heads_dev, tok_ctx), -1e30, jnp.float32)
    key_piece = lax.all_gather(key_mine, "ctx", axis=0, tiled=True)
    value_piece = lax.all_gather(value_mine, "ctx", axis=0, tiled=True)
    scores = (
        jnp.einsum("qhd,kd->hqk", query_heads, key_piece, preferred_element_type=jnp.float32)
        * score_scale
    )
    key_pos = jnp.arange(key_piece.shape[0], dtype=jnp.int32)
    visible = key_pos[None, None, :] <= query_pos[None, :, None]
    block_max = jnp.max(jnp.where(visible, scores, -1e30), axis=2)
    new_running = jnp.maximum(running, block_max)
    weights = jnp.where(visible, jnp.exp(scores - new_running[:, :, None]), 0.0)
    denom = jnp.sum(weights, axis=2)
    accumulated = jnp.einsum(
        "hqk,kd->hqd", weights.astype(jnp.bfloat16), value_piece, preferred_element_type=jnp.float32
    )
    attn_heads = (accumulated / denom[:, :, None]).astype(jnp.bfloat16)
    attn = jnp.transpose(attn_heads, (1, 0, 2)).reshape(tok_ctx, heads_dev * HEAD)
    row_total = resid.shape[0]
    head_mix = lax.psum_scatter(
        jnp.dot(attn, out_proj, preferred_element_type=jnp.float32).astype(jnp.bfloat16),
        "tp",
        scatter_dimension=0,
        tiled=True,
    ).astype(jnp.float32)
    stream = resid.astype(jnp.float32) + head_mix
    normed = (
        stream * lax.rsqrt(jnp.mean(stream * stream, axis=1, keepdims=True) + 1e-06) * norm_gain
    ).astype(jnp.bfloat16)
    exp_dev, ff_dev = w_gate.shape[0], w_gate.shape[1]
    experts_all = exp_dev * groups
    hits = expert_ids[:, :, None] == jnp.arange(experts_all, dtype=jnp.int32)[None, None, :]
    weight_rows = jnp.sum(jnp.where(hits, gates[:, :, None], 0.0), axis=1)
    both = ("ctx", "tp")
    weight_all = lax.all_gather(weight_rows, both, axis=0, tiled=True)
    weight_mine = lax.dynamic_slice_in_dim(
        weight_all, lax.axis_index("ctx") * exp_dev, exp_dev, 1
    )
    weight = jnp.repeat(weight_mine, ff_dev, axis=1)
    cot = lax.all_gather(cotangent, both, axis=0, tiled=True)
    rows = lax.all_gather(normed, both, axis=0, tiled=True)
    wide = exp_dev * ff_dev
    gate_w = w_gate.reshape(wide, D)
    up_w = w_up.reshape(wide, D)
    down_w = w_down.reshape(wide, D)
    f32 = jnp.float32
    back_act = jnp.einsum("td,fd->tf", cot, down_w, preferred_element_type=f32) * weight
    gate_val = jnp.einsum("td,fd->tf", rows, gate_w, preferred_element_type=f32)
    up_val = jnp.einsum("td,fd->tf", rows, up_w, preferred_element_type=f32)
    sigmoid_val = jax.nn.sigmoid(gate_val)
    silu_val = gate_val * sigmoid_val
    activated = (silu_val * up_val * weight).astype(jnp.bfloat16)
    partial = jnp.dot(activated, down_w, preferred_element_type=f32).astype(jnp.bfloat16)
    combined = lax.psum_scatter(partial, both, scatter_dimension=0, tiled=True)
    d_gate = (back_act * up_val * sigmoid_val * (1.0 + gate_val * (1.0 - sigmoid_val))).astype(
        jnp.bfloat16
    )
    d_up = (back_act * silu_val).astype(jnp.bfloat16)

    def grad(left, right):
        out = jnp.einsum("tf,td->fd", left, right, preferred_element_type=f32)
        return out.astype(jnp.bfloat16).reshape(exp_dev, ff_dev, D)

    grad_down = grad(activated, cot)
    grad_gate = grad(d_gate, rows)
    grad_up = grad(d_up, rows)
    layer_out = (stream + combined.astype(f32)).astype(jnp.bfloat16)
    return (layer_out, grad_gate, grad_up, grad_down)


def solution(mesh):
    in_specs = (
        P("ctx", "tp"),
        P("ctx", None),
        P("ctx", None),
        P(("ctx", "tp"), None),
        P("tp", None),
        P(),
        P(("ctx", "tp"), None),
        P(("ctx", "tp"), None),
        P("ctx", "tp", None),
        P("ctx", "tp", None),
        P("ctx", "tp", None),
        P(("ctx", "tp"), None),
    )
    out_specs = (
        P(("ctx", "tp"), None),
        P("ctx", "tp", None),
        P("ctx", "tp", None),
        P("ctx", "tp", None),
    )
    return jax.shard_map(shards, mesh=mesh, in_specs=in_specs, out_specs=out_specs, check_vma=False)
```
